32 devices in a mesh: space: 16 (over z, y, x), sub: 2 (over core).
Axes of the slice: x: 2, y: 2, z: 4, core: 2. Of those that a mesh axis runs over, the one named last changes fastest.
Arguments:
- mode_rows: float32 [256, 262144], P(None, ('space', 'sub')), as said below
- snapshots: float32 [3, 64, 262144], P(None, None, ('space', 'sub')), as said below
- probe_fields: float32 [128, 262144], P(None, ('space', 'sub')), as said below
- core_factor: float32 [256, 256], replicated, as said below
Outputs:
- new_modes: float32 [256, 262144], P(None, ('space', 'sub'))
- new_core: float32 [256, 256], replicated
- captured: float32 [3, 256, 320], replicated
Inputs may be any that keep to these rules, and one draw needn't show every extreme that they name: `mode_rows`: rows of full rank, entries of order one. `snapshots`: fields of order one. `probe_fields`: fields of order one. `core_factor`: lower triangular with a positive diagonal.
All inputs are finite; a program needn't handle non-finite values.
Results may differ from the reference program's by a relative error of at most 0.0003.
Values sent between devices are 32-bit elements; how exact they have to be, the bound alone decides.
No kernel may reach another device: no remote copies, remote signals or barrier semaphores. Data moves between devices by JAX's collectives and lax.ppermute only.
A program may use at most 128 MiB of HBM per device.

```python
import jax
import jax.numpy as jnp
from jax import lax

K = 256
BATCH = 64
BATCHES = 3
PROBES = 128
TURNS = 2
ROWS = 262144


DECAY_END = 0.03


NOISE_SIZE = 0.2


def shared_modes(key):
    return jax.random.normal(jax.random.fold_in(key, 11), (K, ROWS), jnp.float32)


def shared_fields(key):
    field_count = BATCH * 3 // 2
    return jax.random.normal(jax.random.fold_in(key, 13), (field_count, ROWS), jnp.float32)


def mixed_fields(key, salt, number):
    basis_all = shared_modes(key)
    fields = shared_fields(key)
    field_count = fields.shape[0]
    branch_key = jax.random.fold_in(key, salt)
    picked = jax.random.randint(jax.random.fold_in(branch_key, 1), (number, 4), 0, K)
    amounts = jax.random.normal(jax.random.fold_in(branch_key, 2), (number, 4), jnp.float32)
    steps_along = jnp.arange(field_count, dtype=jnp.float32) / (field_count - 1)
    decay = jnp.exp(steps_along * jnp.log(DECAY_END))
    decay = decay / jnp.sqrt(jnp.sum(decay * decay))
    mixing = jax.random.normal(jax.random.fold_in(branch_key, 4), (number, field_count), jnp.float32) * decay[None, :]
    summed = jax.random.normal(jax.random.fold_in(branch_key, 3), (number, ROWS), jnp.float32) * NOISE_SIZE
    summed = summed + jnp.dot(mixing, fields, precision=lax.Precision.HIGHEST)
    for member in range(4):
        summed = summed + amounts[:, member:member + 1] * basis_all[picked[:, member]]
    return summed


def draw_mode_rows(key, part):
    return shared_modes(key)


def draw_snapshots(key, part):
    return mixed_fields(key, 23, BATCHES * BATCH).reshape(BATCHES, BATCH, ROWS)


def draw_probe_fields(key, part):
    return mixed_fields(key, 37, PROBES)


def draw_core_factor(key, part):
    lowest = jnp.tril(jax.random.normal(jax.random.fold_in(key, 5), (K, K), jnp.float32), -1) * (0.5 / K ** 0.5)
    logs = jax.random.uniform(jax.random.fold_in(key, 6), (K,), jnp.float32, jnp.log(0.5), jnp.log(4.0))
    return lowest + jnp.diag(jnp.exp(logs))


def setup_inputs(seed: int = 0) -> dict:
    seeds = jax.random.split(jax.random.key(seed), 5)
    mode_rows = draw_mode_rows(jax.random.fold_in(seeds[4], 71), 0)
    snapshots = draw_snapshots(jax.random.fold_in(seeds[4], 71), 0)
    probe_fields = draw_probe_fields(jax.random.fold_in(seeds[4], 71), 0)
    core_factor = draw_core_factor(jax.random.fold_in(seeds[4], 71), 0)
    return {"mode_rows": mode_rows, "snapshots": snapshots, "probe_fields": probe_fields, "core_factor": core_factor}


PRECISE = lax.Precision.HIGHEST

def row_inner(left, right):
    return lax.dot_general(left, right, (((1,), (1,)), ((), ())), precision=PRECISE)

def matmul_high(left, right):
    return jnp.dot(left, right, precision=PRECISE)

def update_core(core_now, projected, factor):
    rank_count = core_now.shape[0]
    batch_count = factor.shape[0]
    upper = jnp.concatenate([core_now, projected], axis=1)
    bottom = jnp.concatenate([jnp.zeros((batch_count, rank_count), jnp.float32), factor.T], axis=1)
    stacked = jnp.concatenate([upper, bottom], axis=0)
    squared = matmul_high(stacked, stacked.T)
    rotation = jnp.eye(rank_count + batch_count, rank_count, dtype=jnp.float32)
    for sweep_index in range(TURNS):
        rotation = matmul_high(squared, rotation)
        lowered = jnp.linalg.cholesky(matmul_high(rotation.T, rotation))
        rotation = jax.scipy.linalg.solve_triangular(lowered, rotation.T, lower=True).T
    fresh_core = jnp.linalg.cholesky(matmul_high(rotation.T, matmul_high(squared, rotation)))
    return (rotation, fresh_core)

def reference(mode_rows, snapshots, probe_fields, core_factor):
    volume = 1.0 / ROWS
    window = jnp.concatenate([snapshots.reshape(BATCHES * BATCH, ROWS), probe_fields], axis=0)
    captured = []
    basis_now = mode_rows
    core_now = core_factor
    for batch_index in range(BATCHES):
        incoming = snapshots[batch_index]
        projected = row_inner(basis_now, incoming) * volume
        residual = incoming - matmul_high(projected.T, basis_now)
        factor = jnp.linalg.cholesky(row_inner(residual, residual) * volume)
        orthogonal = jax.scipy.linalg.solve_triangular(factor, residual, lower=True)
        rotation, core_now = update_core(core_now, projected, factor)
        basis_now = matmul_high(rotation.T, jnp.concatenate([basis_now, orthogonal], axis=0))
        captured.append(row_inner(basis_now, window) * volume)
    return (basis_now, core_now, jnp.stack(captured))
```

```python
import functools

import jax
import jax.numpy as jnp
from jax import lax
from jax.experimental import pallas as pl
from jax.experimental.pallas import tpu as pltpu
from jax.sharding import PartitionSpec as P

TURNS = 2
AXES = ("space", "sub")
FULL = lax.Precision.HIGHEST
LANES = 128
GROUP = 8
PANEL = 64


def nn(left, right):
    return lax.dot_general(
        left, right, (((1,), (0,)), ((), ())), precision=FULL, preferred_element_type=jnp.float32
    )


def nt(left, right):
    return lax.dot_general(
        left, right, (((1,), (1,)), ((), ())), precision=FULL, preferred_element_type=jnp.float32
    )


def tn(left, right):
    return lax.dot_general(
        left, right, (((0,), (0,)), ((), ())), precision=FULL, preferred_element_type=jnp.float32
    )


def wide(column, order):
    return jnp.concatenate([column] * (order // LANES), axis=1)


def inverse_factor(matrix):
    order = matrix.shape[0]
    lane = lax.broadcasted_iota(jnp.int32, (GROUP, order), 1)
    row = lax.broadcasted_iota(jnp.int32, (GROUP, order), 0)
    row_one = lax.broadcasted_iota(jnp.int32, (GROUP, LANES), 0)
    finished = []
    groups = PANEL // GROUP
    for start in range(0, order, PANEL):
        finish = start + PANEL
        held = [matrix[g * GROUP:(g + 1) * GROUP, :] for g in range(groups)]
        panel = []
        for g0 in range(groups):
            first = start + g0 * GROUP
            spread = [
                [
                    jnp.broadcast_to(held[g][:, first + j:first + j + 1], (GROUP, LANES))
                    for g in range(g0, groups)
                ]
                for j in range(GROUP)
            ]
            inside = (lane >= first) & (lane < first + GROUP)
            held[g0] = jnp.where(inside, jnp.where(lane - first == row, 1.0, 0.0), held[g0])
            for g in range(g0 + 1, groups):
                held[g] = jnp.where(inside, 0.0, held[g])
            pivot_column = jnp.ones((GROUP, LANES), jnp.float32)
            factors = []
            for j in range(GROUP):
                pivot = jnp.broadcast_to(spread[j][0][j:j + 1, :], (GROUP, LANES))
                inverse = pltpu.reciprocal(pivot, approx=True)
                inverse = inverse * (2.0 - pivot * inverse)
                pivot_column = jnp.where(row_one == j, pivot, pivot_column)
                factor = [block * inverse for block in spread[j]]
                for later in range(j + 1, GROUP):
                    across = jnp.broadcast_to(spread[later][0][j:j + 1, :], (GROUP, LANES))
                    for t in range(groups - g0):
                        spread[later][t] = spread[later][t] - factor[t] * across
                factor[0] = jnp.where(row_one > j, factor[0], 0.0)
                factors.append(factor)
            for j in range(GROUP):
                pivot_row = jnp.broadcast_to(held[g0][j:j + 1, :], (GROUP, order))
                for t in range(groups - g0):
                    held[g0 + t] = held[g0 + t] - wide(factors[j][t], order) * pivot_row
            panel.append(held[g0] * wide(lax.rsqrt(pivot_column), order))
        finished.extend(panel)
        if finish < order:
            scaled = jnp.concatenate(
                [
                    jnp.where((lane >= start + GROUP * (g + 1)) & (lane < finish), 0.0, panel[g])
                    for g in range(groups)
                ],
                axis=0,
            )
            rest = matrix[PANEL:, :]
            rest_lane = lax.broadcasted_iota(jnp.int32, rest.shape, 1)
            rest = jnp.where((rest_lane >= start) & (rest_lane < finish), 0.0, rest)
            matrix = rest - tn(scaled[:, finish:], scaled)
    lowered = jnp.concatenate(finished, axis=0)
    lane = lax.broadcasted_iota(jnp.int32, lowered.shape, 1)
    row = lax.broadcasted_iota(jnp.int32, lowered.shape, 0)
    return jnp.where(lane <= row, lowered, 0.0)


def lower_factor(matrix):
    lowered = nt(matrix, inverse_factor(matrix))
    lane = lax.broadcasted_iota(jnp.int32, lowered.shape, 1)
    row = lax.broadcasted_iota(jnp.int32, lowered.shape, 0)
    return jnp.where(lane <= row, lowered, 0.0)


def split(values):
    high = values.astype(jnp.bfloat16)
    low = (values - high.astype(jnp.float32)).astype(jnp.bfloat16)
    return high, low


def nt_pass(left, right):
    return lax.dot_general(
        left, right, (((1,), (1,)), ((), ())), preferred_element_type=jnp.float32
    )


def packed_rows(rank, snap_count, batches):
    own = 3 * (rank // 2)
    return own + (rank + snap_count) * (batches - 1) + (rank + snap_count) // 2


def fold(block):
    half = block.shape[0] // 2
    return jnp.concatenate([block[:half, :LANES // 2], block[half:, :LANES // 2]], axis=1)


def unfold(block):
    zeros = jnp.zeros((block.shape[0], LANES // 2), jnp.float32)
    return jnp.concatenate(
        [
            jnp.concatenate([block[:, :LANES // 2], zeros], axis=1),
            jnp.concatenate([block[:, LANES // 2:], zeros], axis=1),
        ],
        axis=0,
    )


def gram_kernel(scale, modes_ref, snaps_ref, probes_ref, packed_ref, modes_out, snaps_out):
    step = pl.program_id(0)

    @pl.when(step == 0)
    def _():
        modes_out[...] = jnp.zeros_like(modes_out)
        snaps_out[...] = jnp.zeros_like(snaps_out)

    count, width, columns = snaps_ref.shape
    probe_count = probes_ref.shape[0]
    spare = LANES - width
    pieces = []
    for batch in range(count):
        pieces.append(snaps_ref[batch])
        taken = min(max(probe_count - batch * spare, 0), spare)
        if taken:
            pieces.append(probes_ref[batch * spare:batch * spare + taken, :])
        if taken < spare:
            pieces.append(jnp.zeros((spare - taken, columns), jnp.float32))
    high, low = split(modes_ref[...])
    field_high, field_low = split(jnp.concatenate(pieces, axis=0))
    all_high = jnp.concatenate([high, field_high], axis=0)
    all_low = jnp.concatenate([low, field_low], axis=0)
    modes_out[...] += nt_pass(high, all_high) + (nt_pass(high, all_low) + nt_pass(low, all_high))
    snap_high, snap_low = split(snaps_ref[...].reshape(count * width, columns))
    snaps_out[...] += nt_pass(snap_high, field_high) + (
        nt_pass(snap_high, field_low) + nt_pass(snap_low, field_high)
    )

    @pl.when(step == pl.num_programs(0) - 1)
    def _():
        rank = modes_ref.shape[0]
        half = rank // 2
        blocks = [
            modes_out[:half, :half],
            modes_out[half:, :half],
            modes_out[half:, half:rank],
        ]
        for batch in range(count):
            tile = slice(rank + batch * LANES, rank + (batch + 1) * LANES)
            block = modes_out[:, tile]
            blocks.append(block if batch + 1 < count else fold(block))
        for batch in range(count):
            block = snaps_out[:, batch * LANES:(batch + 1) * LANES]
            blocks.append(block if batch + 1 < count else fold(block))
        at = 0
        for block in blocks:
            packed_ref[at:at + block.shape[0], :] = block * scale
            at += block.shape[0]


def local_grams(modes, snaps, probes, scale):
    rank, columns = modes.shape
    count, width, _ = snaps.shape
    probe_count = probes.shape[0]
    fields = count * LANES
    tile = 1024
    rows = packed_rows(rank, count * width, count)
    return pl.pallas_call(
        functools.partial(gram_kernel, scale),
        grid=(columns // tile,),
        in_specs=[
            pl.BlockSpec((rank, tile), lambda i: (0, i)),
            pl.BlockSpec((count, width, tile), lambda i: (0, 0, i)),
            pl.BlockSpec((probe_count, tile), lambda i: (0, i)),
        ],
        out_specs=pl.BlockSpec((rows, LANES), lambda i: (0, 0)),
        out_shape=jax.ShapeDtypeStruct((rows, LANES), jnp.float32),
        scratch_shapes=[
            pltpu.VMEM((rank, rank + fields), jnp.float32),
            pltpu.VMEM((count * width, fields), jnp.float32),
        ],
        compiler_params=pltpu.CompilerParams(vmem_limit_bytes=48 << 20),
        name="grams",
    )(modes, snaps, probes)


def sum_over_devices(part, size):
    def swap(value, bit):
        return lax.ppermute(value, AXES, [(i, i ^ bit) for i in range(size)])

    bits = size.bit_length() - 1
    if size != 1 << bits or bits < 2:
        return lax.psum(part, AXES)
    odd = lax.rem(lax.axis_index(AXES), 2) == 1
    half = part.shape[0] // 2
    low, high = part[:half], part[half:]
    part = jnp.where(odd, high, low) + swap(jnp.where(odd, low, high), 1)
    order = list(range(1, bits))
    chunk = -(-half // (3 * GROUP)) * GROUP
    chunks = [part[at:at + chunk] for at in range(0, half, chunk)]
    for turn in range(bits - 1):
        chunks = [
            piece + swap(piece, 1 << order[(turn + number) % len(order)])
            for number, piece in enumerate(chunks)
        ]
    part = jnp.concatenate(chunks, axis=0)
    other = swap(part, 1)
    return jnp.concatenate([jnp.where(odd, other, part), jnp.where(odd, part, other)], axis=0)


def first_lanes(values, width):
    lane = lax.broadcasted_iota(jnp.int32, values.shape, 1)
    return jnp.where(lane < width, values, 0.0)


def product(left, right, across):
    dims = (((1,), (1 if across else 0,)), ((), ()))

    def one(a, b):
        return lax.dot_general(a, b, dims, preferred_element_type=jnp.float32)

    return one(left[0], right[0]) + (one(left[0], right[1]) + one(left[1], right[0]))


def core_kernel(
    packed_ref, core_ref, mix_ref, core_out, captured_ref, energy_ref, norms_ref, inner_ref, snaps_ref, kept_ref
):
    rank = core_ref.shape[0]
    batches = captured_ref.shape[0]
    width = snaps_ref.shape[0] // batches
    probes = captured_ref.shape[2] - batches * width
    half = rank // 2
    norms_ref[:half, :half] = packed_ref[:half, :]
    norms_ref[half:, :half] = packed_ref[half:rank, :]
    norms_ref[:half, half:] = packed_ref[half:rank, :].T
    norms_ref[half:, half:] = packed_ref[rank:rank + half, :]
    at = rank + half
    for target_ref in (inner_ref, snaps_ref):
        count = target_ref.shape[0]
        for batch in range(batches):
            tile = slice(batch * LANES, (batch + 1) * LANES)
            if batch + 1 < batches:
                target_ref[:, tile] = packed_ref[at:at + count, :]
                at += count
            else:
                target_ref[:, tile] = unfold(packed_ref[at:at + count // 2, :])
                at += count // 2
    energy_ref[...] = nt(core_ref[...], core_ref[...])
    lane = lax.broadcasted_iota(jnp.int32, kept_ref.shape, 1)
    row = lax.broadcasted_iota(jnp.int32, kept_ref.shape, 0)
    kept_ref[...] = jnp.where(lane == row, 1.0, 0.0)
    spare = jnp.zeros((LANES - width, LANES), jnp.float32)

    def absorb(batch, carry):
        tile = pl.ds(pl.multiple_of(batch * LANES, LANES), LANES)
        own_rows = pl.ds(pl.multiple_of(batch * width, GROUP), width)
        own = jnp.concatenate([first_lanes(snaps_ref[own_rows, tile], width), spare], axis=0)
        projected = first_lanes(inner_ref[:, tile], width)
        projected_s = split(projected)
        norms = split(norms_ref[...])
        crossed = tn(projected, projected)
        residual = own - crossed - crossed + tn(projected, product(norms, projected_s, False))
        residual_s = split(residual)
        top = energy_ref[...] + product(projected_s, projected_s, True)
        top_s = split(top)
        coupling_s = split(product(projected_s, residual_s, False))
        gram = product(top_s, top_s, True) + product(coupling_s, projected_s, True)
        inverse = split(inverse_factor(gram))
        first_rows = split(product(inverse, top_s, False))
        first_low = split(product(inverse, projected_s, False))
        turned_rows = product(first_rows, top_s, False) + product(first_low, coupling_s, True)
        turned_low = product(first_rows, projected_s, False) + product(first_low, residual_s, False)
        gram = nt(turned_rows, turned_rows) + nt(nn(turned_low, residual), turned_low)
        inverse = inverse_factor(gram)
        rows = nn(inverse, turned_rows)
        low = nn(inverse, turned_low)
        rows_s = split(rows)
        low_s = split(low)
        low_residual = product(low_s, residual_s, False)
        applied_rows = product(rows_s, top_s, False) + product(low_s, coupling_s, True)
        applied_low = product(rows_s, projected_s, False) + low_residual
        energy_ref[...] = product(split(applied_rows), rows_s, True) + product(
            split(applied_low), split(low_residual), True
        )
        old = split(rows - product(low_s, projected_s, True))
        with_window = jnp.concatenate(
            [snaps_ref[own_rows, :], jnp.zeros((LANES - width, snaps_ref.shape[1]), jnp.float32)], axis=0
        )
        inner_ref[...] = product(old, split(inner_ref[...]), False) + product(low_s, split(with_window), False)
        across = product(old, norms, False) + product(low_s, projected_s, True)
        norms_ref[...] = product(split(across), old, True) + product(
            split(first_lanes(inner_ref[:, tile], width)), low_s, True
        )
        kept_ref[...] = product(old, split(kept_ref[...]), False)
        kept_ref[:, pl.ds(pl.multiple_of(rank + batch * LANES, LANES), LANES)] = low
        captured_ref[batch] = jnp.concatenate(
            [inner_ref[:, b * LANES:b * LANES + width] for b in range(batches)]
            + [
                inner_ref[:, b * LANES + width:(b + 1) * LANES]
                for b in range(probes // (LANES - width))
            ],
            axis=1,
        )
        return carry

    lax.fori_loop(0, batches, absorb, 0)
    mix_ref[...] = jnp.concatenate(
        [kept_ref[:, :rank]]
        + [kept_ref[:, rank + b * LANES:rank + b * LANES + width] for b in range(batches)],
        axis=1,
    )
    core_out[...] = lower_factor(energy_ref[...])


def small_algebra(packed, core, batches, width, probes):
    rank = core.shape[0]
    snap_count = batches * width
    columns = batches * LANES
    return pl.pallas_call(
        core_kernel,
        out_shape=[
            jax.ShapeDtypeStruct((rank, rank + snap_count), jnp.float32),
            jax.ShapeDtypeStruct((rank, rank), jnp.float32),
            jax.ShapeDtypeStruct((batches, rank, snap_count + probes), jnp.float32),
        ],
        scratch_shapes=[
            pltpu.VMEM((rank, rank), jnp.float32),
            pltpu.VMEM((rank, rank), jnp.float32),
            pltpu.VMEM((rank, columns), jnp.float32),
            pltpu.VMEM((snap_count, columns), jnp.float32),
            pltpu.VMEM((rank, rank + columns), jnp.float32),
        ],
        compiler_params=pltpu.CompilerParams(vmem_limit_bytes=48 << 20),
        name="core_updates",
    )(packed, core)


def apply_kernel(mix_ref, modes_ref, snaps_ref, out_ref):
    count, width, columns = snaps_ref.shape
    rows = jnp.concatenate([modes_ref[...], snaps_ref[...].reshape(count * width, columns)], axis=0)
    high, low = split(rows)
    mix_high, mix_low = split(mix_ref[...])

    def one(left, right):
        return lax.dot_general(
            left, right, (((1,), (0,)), ((), ())), preferred_element_type=jnp.float32
        )

    out_ref[...] = one(mix_high, high) + (one(mix_high, low) + one(mix_low, high))


def apply_mix(mix, modes, snaps):
    rank, columns = modes.shape
    count, width, _ = snaps.shape
    tile = 1024
    return pl.pallas_call(
        apply_kernel,
        grid=(columns // tile,),
        in_specs=[
            pl.BlockSpec(mix.shape, lambda i: (0, 0)),
            pl.BlockSpec((rank, tile), lambda i: (0, i)),
            pl.BlockSpec((count, width, tile), lambda i: (0, 0, i)),
        ],
        out_specs=pl.BlockSpec((rank, tile), lambda i: (0, i)),
        out_shape=jax.ShapeDtypeStruct((rank, columns), jnp.float32),
        compiler_params=pltpu.CompilerParams(vmem_limit_bytes=48 << 20),
        name="new_basis",
    )(mix, modes, snaps)


def body(modes, snaps, probes, core, *, devices):
    rank, columns = modes.shape
    batches, width, _ = snaps.shape
    scale = 1.0 / (columns * devices)
    packed = sum_over_devices(local_grams(modes, snaps, probes, scale), devices)
    mix, new_core, captured = small_algebra(packed, core, batches, width, probes.shape[0])
    return apply_mix(mix, modes, snaps), new_core, captured


def solution(mesh):
    devices = mesh.shape["space"] * mesh.shape["sub"]
    return jax.shard_map(
        functools.partial(body, devices=devices),
        mesh=mesh,
        in_specs=(P(None, AXES), P(None, None, AXES), P(None, AXES), P()),
        out_specs=(P(None, AXES), P(), P()),
        check_vma=False,
    )
```

```python
import functools

import jax
import jax.numpy as jnp
from jax import lax
from jax.experimental import pallas as pl
from jax.experimental.pallas import tpu as pltpu
from jax.sharding import PartitionSpec as P

TURNS = 2
AXES = ("space", "sub")
FULL = lax.Precision.HIGHEST
LANES = 128
GROUP = 8
PANEL = 32
FINAL_PANEL = 64


def nn(left, right):
    return lax.dot_general(
        left, right, (((1,), (0,)), ((), ())), precision=FULL, preferred_element_type=jnp.float32
    )


def nt(left, right):
    return lax.dot_general(
        left, right, (((1,), (1,)), ((), ())), precision=FULL, preferred_element_type=jnp.float32
    )


def tn(left, right):
    return lax.dot_general(
        left, right, (((0,), (0,)), ((), ())), precision=FULL, preferred_element_type=jnp.float32
    )


def wide(column, order):
    return jnp.concatenate([column] * (order // LANES), axis=1)


def eliminate_panel(block, start, inverting):
    size, order = block.shape
    lane = lax.broadcasted_iota(jnp.int32, (GROUP, order), 1)
    row = lax.broadcasted_iota(jnp.int32, (GROUP, order), 0)
    row_one = lax.broadcasted_iota(jnp.int32, (GROUP, LANES), 0)
    groups = size // GROUP
    held = [block[g * GROUP:(g + 1) * GROUP, :] for g in range(groups)]
    panel = []

    def spread(first, g0):
        return [
            [
                jnp.broadcast_to(held[g][:, first + j:first + j + 1], (GROUP, LANES))
                for g in range(g0, groups)
            ]
            for j in range(GROUP)
        ]

    own = spread(start, 0)
    for g0 in range(groups):
        first = start + g0 * GROUP
        ahead = spread(first + GROUP, g0) if g0 + 1 < groups else []
        if inverting:
            inside = (lane >= first) & (lane < first + GROUP)
            held[g0] = jnp.where(inside, jnp.where(lane - first == row, 1.0, 0.0), held[g0])
            for g in range(g0 + 1, groups):
                held[g] = jnp.where(inside, 0.0, held[g])
        pivot_column = jnp.ones((GROUP, LANES), jnp.float32)
        factors = []
        for j in range(GROUP):
            pivot = jnp.broadcast_to(own[j][0][j:j + 1, :], (GROUP, LANES))
            inverse = pltpu.reciprocal(pivot, approx=True)
            pivot_column = jnp.where(row_one == j, pivot, pivot_column)
            factor = [column * inverse for column in own[j]]
            for column in own[j + 1:] + ahead:
                across = jnp.broadcast_to(column[0][j:j + 1, :], (GROUP, LANES))
                for t in range(groups - g0):
                    column[t] = column[t] - factor[t] * across
            factor[0] = jnp.where(row_one > j, factor[0], 0.0)
            factors.append(factor)
        for j in range(GROUP):
            pivot_row = jnp.broadcast_to(held[g0][j:j + 1, :], (GROUP, order))
            for t in range(groups - g0):
                held[g0 + t] = held[g0 + t] - wide(factors[j][t], order) * pivot_row
        panel.append(held[g0] * wide(lax.rsqrt(pivot_column), order))
        own = [column[1:] for column in ahead]
        yield
    if inverting:
        panel = [
            jnp.where((lane >= start + GROUP * (g + 1)) & (lane < start + size), 0.0, panel[g])
            for g in range(groups)
        ]
    return jnp.concatenate(panel, axis=0)


def finish(steps):
    while True:
        try:
            next(steps)
        except StopIteration as done:
            return done.value


def stacked_square(panel, begin):
    high = panel.astype(jnp.bfloat16)
    left = panel - high.astype(jnp.float32)
    mid = left.astype(jnp.bfloat16)
    low = (left - mid.astype(jnp.float32)).astype(jnp.bfloat16)
    first = jnp.concatenate([high, high, mid, mid, high, low], axis=0)
    second = jnp.concatenate([high, mid, high, mid, low, high], axis=0)
    return lax.dot_general(
        first[:, begin:], second, (((0,), (0,)), ((), ())), preferred_element_type=jnp.float32
    )


def inverse_factor(matrix):
    order = matrix.shape[0]
    finished = []
    for start in range(0, order, PANEL):
        end = start + PANEL
        panel = finish(eliminate_panel(matrix[:PANEL, :], start, True))
        finished.append(panel)
        if end < order:
            rest = matrix[PANEL:, :]
            rest_lane = lax.broadcasted_iota(jnp.int32, rest.shape, 1)
            rest = jnp.where((rest_lane >= start) & (rest_lane < end), 0.0, rest)
            matrix = rest - stacked_square(panel, end)
    lowered = jnp.concatenate(finished, axis=0)
    lane = lax.broadcasted_iota(jnp.int32, lowered.shape, 1)
    row = lax.broadcasted_iota(jnp.int32, lowered.shape, 0)
    return jnp.where(lane <= row, lowered, 0.0)


def split(values):
    high = values.astype(jnp.bfloat16)
    low = (values - high.astype(jnp.float32)).astype(jnp.bfloat16)
    return high, low


def nt_pass(left, right):
    return lax.dot_general(
        left, right, (((1,), (1,)), ((), ())), preferred_element_type=jnp.float32
    )


def packed_rows(rank, snap_count, batches):
    own = 3 * (rank // 2)
    return own + (rank + snap_count) * (batches - 1) + (rank + snap_count) // 2


def fold(block):
    half = block.shape[0] // 2
    return jnp.concatenate([block[:half, :LANES // 2], block[half:, :LANES // 2]], axis=1)


def unfold(block):
    zeros = jnp.zeros((block.shape[0], LANES // 2), jnp.float32)
    return jnp.concatenate(
        [
            jnp.concatenate([block[:, :LANES // 2], zeros], axis=1),
            jnp.concatenate([block[:, LANES // 2:], zeros], axis=1),
        ],
        axis=0,
    )


def gram_kernel(scale, modes_ref, snaps_ref, probes_ref, packed_ref, modes_out, snaps_out):
    step = pl.program_id(0)

    @pl.when(step == 0)
    def _():
        modes_out[...] = jnp.zeros_like(modes_out)
        snaps_out[...] = jnp.zeros_like(snaps_out)

    count, width, columns = snaps_ref.shape
    probe_count = probes_ref.shape[0]
    spare = LANES - width
    pieces = []
    for batch in range(count):
        pieces.append(snaps_ref[batch])
        taken = min(max(probe_count - batch * spare, 0), spare)
        if taken:
            pieces.append(probes_ref[batch * spare:batch * spare + taken, :])
        if taken < spare:
            pieces.append(jnp.zeros((spare - taken, columns), jnp.float32))
    high, low = split(modes_ref[...])
    field_high, field_low = split(jnp.concatenate(pieces, axis=0))
    all_high = jnp.concatenate([high, field_high], axis=0)
    all_low = jnp.concatenate([low, field_low], axis=0)
    modes_out[...] += nt_pass(high, all_high) + (nt_pass(high, all_low) + nt_pass(low, all_high))
    snap_high, snap_low = split(snaps_ref[...].reshape(count * width, columns))
    snaps_out[...] += nt_pass(snap_high, field_high) + (
        nt_pass(snap_high, field_low) + nt_pass(snap_low, field_high)
    )

    @pl.when(step == pl.num_programs(0) - 1)
    def _():
        rank = modes_ref.shape[0]
        half = rank // 2
        blocks = [
            modes_out[:half, :half],
            modes_out[half:, :half],
            modes_out[half:, half:rank],
        ]
        for batch in range(count):
            tile = slice(rank + batch * LANES, rank + (batch + 1) * LANES)
            block = modes_out[:, tile]
            blocks.append(block if batch + 1 < count else fold(block))
        for batch in range(count):
            block = snaps_out[:, batch * LANES:(batch + 1) * LANES]
            blocks.append(block if batch + 1 < count else fold(block))
        at = 0
        for block in blocks:
            packed_ref[at:at + block.shape[0], :] = block * scale
            at += block.shape[0]


def local_grams(modes, snaps, probes, scale):
    rank, columns = modes.shape
    count, width, _ = snaps.shape
    probe_count = probes.shape[0]
    fields = count * LANES
    tile = 1024
    rows = packed_rows(rank, count * width, count)
    return pl.pallas_call(
        functools.partial(gram_kernel, scale),
        grid=(columns // tile,),
        in_specs=[
            pl.BlockSpec((rank, tile), lambda i: (0, i)),
            pl.BlockSpec((count, width, tile), lambda i: (0, 0, i)),
            pl.BlockSpec((probe_count, tile), lambda i: (0, i)),
        ],
        out_specs=pl.BlockSpec((rows, LANES), lambda i: (0, 0)),
        out_shape=jax.ShapeDtypeStruct((rows, LANES), jnp.float32),
        scratch_shapes=[
            pltpu.VMEM((rank, rank + fields), jnp.float32),
            pltpu.VMEM((count * width, fields), jnp.float32),
        ],
        compiler_params=pltpu.CompilerParams(vmem_limit_bytes=48 << 20),
        name="grams",
    )(modes, snaps, probes)


def sum_over_devices(part, size):
    def swap(value, bit):
        return lax.ppermute(value, AXES, [(i, i ^ bit) for i in range(size)])

    bits = size.bit_length() - 1
    if size != 1 << bits or bits < 2:
        return lax.psum(part, AXES)
    odd = lax.rem(lax.axis_index(AXES), 2) == 1
    half = part.shape[0] // 2
    low, high = part[:half], part[half:]
    part = jnp.where(odd, high, low) + swap(jnp.where(odd, low, high), 1)
    order = list(range(1, bits))
    chunk = -(-half // (3 * GROUP)) * GROUP
    chunks = [part[at:at + chunk] for at in range(0, half, chunk)]
    for turn in range(bits - 1):
        chunks = [
            piece + swap(piece, 1 << order[(turn + number) % len(order)])
            for number, piece in enumerate(chunks)
        ]
    part = jnp.concatenate(chunks, axis=0)
    other = swap(part, 1)
    return jnp.concatenate([jnp.where(odd, other, part), jnp.where(odd, part, other)], axis=0)


def first_lanes(values, width):
    lane = lax.broadcasted_iota(jnp.int32, values.shape, 1)
    return jnp.where(lane < width, values, 0.0)


def product(left, right, across):
    dims = (((1,), (1 if across else 0,)), ((), ()))

    def one(a, b):
        return lax.dot_general(a, b, dims, preferred_element_type=jnp.float32)

    return one(left[0], right[0]) + (one(left[0], right[1]) + one(left[1], right[0]))


def core_kernel(
    packed_ref, core_ref, mix_ref, energy_out, captured_ref, energy_ref, norms_ref, inner_ref, snaps_ref, kept_ref
):
    rank = core_ref.shape[0]
    batches = captured_ref.shape[0]
    width = snaps_ref.shape[0] // batches
    probes = captured_ref.shape[2] - batches * width
    half = rank // 2
    norms_ref[:half, :half] = packed_ref[:half, :]
    norms_ref[half:, :half] = packed_ref[half:rank, :]
    norms_ref[:half, half:] = packed_ref[half:rank, :].T
    norms_ref[half:, half:] = packed_ref[rank:rank + half, :]
    at = rank + half
    for target_ref in (inner_ref, snaps_ref):
        count = target_ref.shape[0]
        for batch in range(batches):
            tile = slice(batch * LANES, (batch + 1) * LANES)
            if batch + 1 < batches:
                target_ref[:, tile] = packed_ref[at:at + count, :]
                at += count
            else:
                target_ref[:, tile] = unfold(packed_ref[at:at + count // 2, :])
                at += count // 2
    energy_ref[...] = nt(core_ref[...], core_ref[...])
    lane = lax.broadcasted_iota(jnp.int32, kept_ref.shape, 1)
    row = lax.broadcasted_iota(jnp.int32, kept_ref.shape, 0)
    kept_ref[...] = jnp.where(lane == row, 1.0, 0.0)
    spare = jnp.zeros((LANES - width, LANES), jnp.float32)

    def absorb(batch, carry):
        tile = pl.ds(pl.multiple_of(batch * LANES, LANES), LANES)
        own_rows = pl.ds(pl.multiple_of(batch * width, GROUP), width)
        own = jnp.concatenate([first_lanes(snaps_ref[own_rows, tile], width), spare], axis=0)
        projected = first_lanes(inner_ref[:, tile], width)
        projected_s = split(projected)
        norms = split(norms_ref[...])
        crossed = tn(projected, projected)
        residual = own - crossed - crossed + tn(projected, product(norms, projected_s, False))
        residual_s = split(residual)
        top = energy_ref[...] + product(projected_s, projected_s, True)
        top_s = split(top)
        coupling_s = split(product(projected_s, residual_s, False))
        gram = product(top_s, top_s, True) + product(coupling_s, projected_s, True)
        inverse = split(inverse_factor(gram))
        first_rows = split(product(inverse, top_s, False))
        first_low = split(product(inverse, projected_s, False))
        turned_rows = product(first_rows, top_s, False) + product(first_low, coupling_s, True)
        turned_low = product(first_rows, projected_s, False) + product(first_low, residual_s, False)
        gram = nt(turned_rows, turned_rows) + nt(nn(turned_low, residual), turned_low)
        inverse = inverse_factor(gram)
        rows = nn(inverse, turned_rows)
        low = nn(inverse, turned_low)
        rows_s = split(rows)
        low_s = split(low)
        low_residual = product(low_s, residual_s, False)
        applied_rows = product(rows_s, top_s, False) + product(low_s, coupling_s, True)
        applied_low = product(rows_s, projected_s, False) + low_residual
        energy_ref[...] = product(split(applied_rows), rows_s, True) + product(
            split(applied_low), split(low_residual), True
        )
        old = split(rows - product(low_s, projected_s, True))
        with_window = jnp.concatenate(
            [snaps_ref[own_rows, :], jnp.zeros((LANES - width, snaps_ref.shape[1]), jnp.float32)], axis=0
        )
        inner_ref[...] = product(old, split(inner_ref[...]), False) + product(low_s, split(with_window), False)
        across = product(old, norms, False) + product(low_s, projected_s, True)
        norms_ref[...] = product(split(across), old, True) + product(
            split(first_lanes(inner_ref[:, tile], width)), low_s, True
        )
        kept_ref[...] = product(old, split(kept_ref[...]), False)
        kept_ref[:, pl.ds(pl.multiple_of(rank + batch * LANES, LANES), LANES)] = low
        captured_ref[batch] = jnp.concatenate(
            [inner_ref[:, b * LANES:b * LANES + width] for b in range(batches)]
            + [
                inner_ref[:, b * LANES + width:(b + 1) * LANES]
                for b in range(probes // (LANES - width))
            ],
            axis=1,
        )
        return carry

    lax.fori_loop(0, batches, absorb, 0)
    mix_ref[...] = jnp.concatenate(
        [kept_ref[:, :rank]]
        + [kept_ref[:, rank + b * LANES:rank + b * LANES + width] for b in range(batches)],
        axis=1,
    )
    energy_out[...] = energy_ref[...]


def small_algebra(packed, core, batches, width, probes):
    rank = core.shape[0]
    snap_count = batches * width
    columns = batches * LANES
    return pl.pallas_call(
        core_kernel,
        out_shape=[
            jax.ShapeDtypeStruct((rank, rank + snap_count), jnp.float32),
            jax.ShapeDtypeStruct((rank, rank), jnp.float32),
            jax.ShapeDtypeStruct((batches, rank, snap_count + probes), jnp.float32),
        ],
        scratch_shapes=[
            pltpu.VMEM((rank, rank), jnp.float32),
            pltpu.VMEM((rank, rank), jnp.float32),
            pltpu.VMEM((rank, columns), jnp.float32),
            pltpu.VMEM((snap_count, columns), jnp.float32),
            pltpu.VMEM((rank, rank + columns), jnp.float32),
        ],
        compiler_params=pltpu.CompilerParams(vmem_limit_bytes=48 << 20),
        name="core_updates",
    )(packed, core)


def apply_kernel(mix_ref, energy_ref, modes_ref, snaps_ref, out_ref, core_ref, mixed_ref, left_ref):
    step = pl.program_id(0)
    count, width, columns = snaps_ref.shape
    rank = energy_ref.shape[0]

    @pl.when(step == 0)
    def _():
        left_ref[...] = energy_ref[...]
        high, low = split(mix_ref[...])
        mixed_ref[0] = high
        mixed_ref[1] = low

    def one(left, right):
        return lax.dot_general(
            left, right, (((1,), (0,)), ((), ())), preferred_element_type=jnp.float32
        )

    def block_of(start):
        end = start + FINAL_PANEL
        steps = eliminate_panel(left_ref[start:end, :], start, False)
        piece = columns // (FINAL_PANEL // GROUP)
        for number in range(FINAL_PANEL // GROUP):
            part = slice(number * piece, (number + 1) * piece)
            rows = jnp.concatenate(
                [modes_ref[:, part], snaps_ref[:, :, part].reshape(count * width, piece)], axis=0
            )
            high, low = split(rows)
            mix_high, mix_low = mixed_ref[0], mixed_ref[1]
            out_ref[:, part] = one(mix_high, high) + (one(mix_high, low) + one(mix_low, high))
            next(steps)
        panel = finish(steps)
        left_ref[start:end, :] = panel
        if end < rank:
            left_ref[end:, :] = left_ref[end:, :] - tn(panel[:, end:], panel)
        else:
            lane = lax.broadcasted_iota(jnp.int32, (rank, rank), 1)
            row = lax.broadcasted_iota(jnp.int32, (rank, rank), 0)
            core_ref[...] = jnp.where(lane >= row, left_ref[...], 0.0).T

    for number in range(rank // FINAL_PANEL):
        pl.when(step == number)(functools.partial(block_of, number * FINAL_PANEL))


def apply_mix(mix, energy, modes, snaps):
    rank, columns = modes.shape
    count, width, _ = snaps.shape
    steps = rank // FINAL_PANEL
    tile = columns // steps
    return pl.pallas_call(
        apply_kernel,
        grid=(steps,),
        in_specs=[
            pl.BlockSpec(mix.shape, lambda i: (0, 0)),
            pl.BlockSpec(energy.shape, lambda i: (0, 0)),
            pl.BlockSpec((rank, tile), lambda i: (0, i)),
            pl.BlockSpec((count, width, tile), lambda i: (0, 0, i)),
        ],
        out_specs=[
            pl.BlockSpec((rank, tile), lambda i: (0, i)),
            pl.BlockSpec((rank, rank), lambda i: (0, 0)),
        ],
        out_shape=[
            jax.ShapeDtypeStruct((rank, columns), jnp.float32),
            jax.ShapeDtypeStruct((rank, rank), jnp.float32),
        ],
        scratch_shapes=[
            pltpu.VMEM((2,) + mix.shape, jnp.bfloat16),
            pltpu.VMEM((rank, rank), jnp.float32),
        ],
        compiler_params=pltpu.CompilerParams(vmem_limit_bytes=48 << 20),
        name="new_basis",
    )(mix, energy, modes, snaps)


def body(modes, snaps, probes, core, *, devices):
    rank, columns = modes.shape
    batches, width, _ = snaps.shape
    scale = 1.0 / (columns * devices)
    packed = sum_over_devices(local_grams(modes, snaps, probes, scale), devices)
    mix, energy, captured = small_algebra(packed, core, batches, width, probes.shape[0])
    new_modes, new_core = apply_mix(mix, energy, modes, snaps)
    return new_modes, new_core, captured


def solution(mesh):
    devices = mesh.shape["space"] * mesh.shape["sub"]
    return jax.shard_map(
        functools.partial(body, devices=devices),
        mesh=mesh,
        in_specs=(P(None, AXES), P(None, None, AXES), P(None, AXES), P()),
        out_specs=(P(None, AXES), P(), P()),
        check_vma=False,
    )
```

```python
import functools

import jax
import jax.numpy as jnp
from jax import lax
from jax.experimental import pallas as pl
from jax.experimental.pallas import tpu as pltpu
from jax.sharding import PartitionSpec as P

TURNS = 2
AXES = ("space", "sub")
FULL = lax.Precision.HIGHEST
LANES = 128
GROUP = 8
PANEL = 32


def nn(left, right):
    return lax.dot_general(
        left, right, (((1,), (0,)), ((), ())), precision=FULL, preferred_element_type=jnp.float32
    )


def nt(left, right):
    return lax.dot_general(
        left, right, (((1,), (1,)), ((), ())), precision=FULL, preferred_element_type=jnp.float32
    )


def tn(left, right):
    return lax.dot_general(
        left, right, (((0,), (0,)), ((), ())), precision=FULL, preferred_element_type=jnp.float32
    )


def wide(column, order):
    return jnp.concatenate([column] * (order // LANES), axis=1)


def eliminate_panel(block, start, inverting):
    size, order = block.shape
    lane = lax.broadcasted_iota(jnp.int32, (GROUP, order), 1)
    row = lax.broadcasted_iota(jnp.int32, (GROUP, order), 0)
    row_one = lax.broadcasted_iota(jnp.int32, (GROUP, LANES), 0)
    groups = size // GROUP
    held = [block[g * GROUP:(g + 1) * GROUP, :] for g in range(groups)]
    panel = []

    def spread(first, g0):
        return [
            [
                jnp.broadcast_to(held[g][:, first + j:first + j + 1], (GROUP, LANES))
                for g in range(g0, groups)
            ]
            for j in range(GROUP)
        ]

    own = spread(start, 0)
    for g0 in range(groups):
        first = start + g0 * GROUP
        ahead = spread(first + GROUP, g0) if g0 + 1 < groups else []
        if inverting:
            inside = (lane >= first) & (lane < first + GROUP)
            held[g0] = jnp.where(inside, jnp.where(lane - first == row, 1.0, 0.0), held[g0])
            for g in range(g0 + 1, groups):
                held[g] = jnp.where(inside, 0.0, held[g])
        pivot_column = jnp.ones((GROUP, LANES), jnp.float32)
        factors = []
        for j in range(GROUP):
            pivot = jnp.broadcast_to(own[j][0][j:j + 1, :], (GROUP, LANES))
            inverse = pltpu.reciprocal(pivot, approx=True)
            pivot_column = jnp.where(row_one == j, pivot, pivot_column)
            factor = [column * inverse for column in own[j]]
            for column in own[j + 1:] + ahead:
                across = jnp.broadcast_to(column[0][j:j + 1, :], (GROUP, LANES))
                for t in range(groups - g0):
                    column[t] = column[t] - factor[t] * across
            factor[0] = jnp.where(row_one > j, factor[0], 0.0)
            factors.append(factor)
        for j in range(GROUP):
            pivot_row = jnp.broadcast_to(held[g0][j:j + 1, :], (GROUP, order))
            for t in range(groups - g0):
                held[g0 + t] = held[g0 + t] - wide(factors[j][t], order) * pivot_row
        panel.append(held[g0] * wide(lax.rsqrt(pivot_column), order))
        own = [column[1:] for column in ahead]
        yield
    if inverting:
        panel = [
            jnp.where((lane >= start + GROUP * (g + 1)) & (lane < start + size), 0.0, panel[g])
            for g in range(groups)
        ]
    return jnp.concatenate(panel, axis=0)


def finish(steps):
    while True:
        try:
            next(steps)
        except StopIteration as done:
            return done.value


def stacked_square(panel, begin):
    high = panel.astype(jnp.bfloat16)
    left = panel - high.astype(jnp.float32)
    mid = left.astype(jnp.bfloat16)
    low = (left - mid.astype(jnp.float32)).astype(jnp.bfloat16)
    first = jnp.concatenate([high, high, mid, mid, high, low], axis=0)
    second = jnp.concatenate([high, mid, high, mid, low, high], axis=0)
    return lax.dot_general(
        first[:, begin:], second, (((0,), (0,)), ((), ())), preferred_element_type=jnp.float32
    )


def inverse_factor(matrix):
    order = matrix.shape[0]
    finished = []
    for start in range(0, order, PANEL):
        end = start + PANEL
        panel = finish(eliminate_panel(matrix[:PANEL, :], start, True))
        finished.append(panel)
        if end < order:
            rest = matrix[PANEL:, :]
            rest_lane = lax.broadcasted_iota(jnp.int32, rest.shape, 1)
            rest = jnp.where((rest_lane >= start) & (rest_lane < end), 0.0, rest)
            matrix = rest - stacked_square(panel, end)
    lowered = jnp.concatenate(finished, axis=0)
    lane = lax.broadcasted_iota(jnp.int32, lowered.shape, 1)
    row = lax.broadcasted_iota(jnp.int32, lowered.shape, 0)
    return jnp.where(lane <= row, lowered, 0.0)


def split(values):
    high = values.astype(jnp.bfloat16)
    low = (values - high.astype(jnp.float32)).astype(jnp.bfloat16)
    return high, low


def nt_pass(left, right):
    return lax.dot_general(
        left, right, (((1,), (1,)), ((), ())), preferred_element_type=jnp.float32
    )


def packed_rows(rank, snap_count, batches):
    own = 3 * (rank // 2)
    rows = own + (rank + snap_count) * (batches - 1) + (rank + snap_count) // 2
    return -(-rows // (8 * GROUP)) * (8 * GROUP)


def fold(block):
    half = block.shape[0] // 2
    return jnp.concatenate([block[:half, :LANES // 2], block[half:, :LANES // 2]], axis=1)


def unfold(block):
    zeros = jnp.zeros((block.shape[0], LANES // 2), jnp.float32)
    return jnp.concatenate(
        [
            jnp.concatenate([block[:, :LANES // 2], zeros], axis=1),
            jnp.concatenate([block[:, LANES // 2:], zeros], axis=1),
        ],
        axis=0,
    )


def gram_kernel(
    scale, modes_ref, snaps_ref, probes_ref, packed_ref, norms_out, cross_out, past_snaps, past_probes, own_out, own_cross, others_out
):
    step = pl.program_id(0)
    sums = (norms_out, cross_out, past_snaps, past_probes, own_out, own_cross, others_out)

    @pl.when(step == 0)
    def _():
        for ref in sums:
            ref[...] = jnp.zeros_like(ref)

    rank, columns = modes_ref.shape
    count, width, _ = snaps_ref.shape
    snap_count = count * width
    probe_count = probes_ref.shape[0]
    high, low = split(modes_ref[...])
    snap_high, snap_low = split(snaps_ref[...].reshape(snap_count, columns))
    probe_high, probe_low = split(probes_ref[...])
    norms_out[...] += nt_pass(high, high)
    cross_out[...] += nt_pass(low, high)
    past_snaps[...] += nt_pass(snap_high, high) + (nt_pass(snap_low, high) + nt_pass(snap_high, low))
    past_probes[...] += nt_pass(probe_high, high) + (nt_pass(probe_low, high) + nt_pass(probe_high, low))
    own_out[...] += nt_pass(snap_high, snap_high)
    own_cross[...] += nt_pass(snap_low, snap_high)
    others_out[...] += nt_pass(snap_high, probe_high) + (
        nt_pass(snap_low, probe_high) + nt_pass(snap_high, probe_low)
    )

    @pl.when(step == pl.num_programs(0) - 1)
    def _():
        half = rank // 2
        spare = LANES - width
        cross = cross_out[...]
        norms = norms_out[...] + (cross + cross.T)
        blocks = [norms[:half, :half], norms[half:, :half], norms[half:, half:]]
        for batch in range(count):
            tile = [past_snaps[batch * width:(batch + 1) * width, :]]
            taken = min(max(probe_count - batch * spare, 0), spare)
            if taken:
                tile.append(past_probes[batch * spare:batch * spare + taken, :])
            if taken < spare:
                tile.append(jnp.zeros((spare - taken, rank), jnp.float32))
            tile = jnp.concatenate(tile, axis=0)
            block = jnp.concatenate([tile[:, :half].T, tile[:, half:].T], axis=0)
            blocks.append(block if batch + 1 < count else fold(block))
        cross = jnp.concatenate(
            [own_cross[...], jnp.zeros((snap_count, rank - snap_count), jnp.float32)], axis=1
        )
        cross = jnp.concatenate([cross, jnp.zeros((rank - snap_count, rank), jnp.float32)], axis=0)
        own = own_out[...] + (own_cross[...] + cross.T[:snap_count, :snap_count])
        for batch in range(count):
            tile = [own[:, batch * width:(batch + 1) * width]]
            taken = min(max(probe_count - batch * spare, 0), spare)
            if taken:
                tile.append(others_out[:, batch * spare:batch * spare + taken])
            if taken < spare:
                tile.append(jnp.zeros((snap_count, spare - taken), jnp.float32))
            block = jnp.concatenate(tile, axis=1)
            blocks.append(block if batch + 1 < count else fold(block))
        at = 0
        for block in blocks:
            packed_ref[at:at + block.shape[0], :] = block * scale
            at += block.shape[0]
        if at < packed_ref.shape[0]:
            packed_ref[at:, :] = jnp.zeros((packed_ref.shape[0] - at, LANES), jnp.float32)


def local_grams(modes, snaps, probes, scale):
    rank, columns = modes.shape
    count, width, _ = snaps.shape
    probe_count = probes.shape[0]
    tile = 1024
    rows = packed_rows(rank, count * width, count)
    return pl.pallas_call(
        functools.partial(gram_kernel, scale),
        grid=(columns // tile,),
        in_specs=[
            pl.BlockSpec((rank, tile), lambda i: (0, i)),
            pl.BlockSpec((count, width, tile), lambda i: (0, 0, i)),
            pl.BlockSpec((probe_count, tile), lambda i: (0, i)),
        ],
        out_specs=pl.BlockSpec((rows, LANES), lambda i: (0, 0)),
        out_shape=jax.ShapeDtypeStruct((rows, LANES), jnp.float32),
        scratch_shapes=[
            pltpu.VMEM(shape, jnp.float32)
            for shape in (
                (rank, rank), (rank, rank), (count * width, rank), (probe_count, rank),
                (count * width, count * width), (count * width, count * width), (count * width, probe_count),
            )
        ],
        compiler_params=pltpu.CompilerParams(vmem_limit_bytes=60 << 20),
        name="grams",
    )(modes, snaps, probes)


def sum_over_devices(part, size):
    def swap(value, mask):
        return lax.ppermute(value, AXES, [(i, i ^ mask) for i in range(size)])

    bits = size.bit_length() - 1
    if size != 1 << bits or bits < 3 or part.shape[0] % (8 * GROUP):
        return lax.psum(part, AXES)
    index = lax.axis_index(AXES)
    odd = lax.rem(index, 2) == 1
    half = part.shape[0] // 2
    low, high = part[:half], part[half:]
    part = jnp.where(odd, high, low) + swap(jnp.where(odd, low, high), 1)
    place = lax.rem(lax.div(index, 2), 4)
    rows = half // 4

    def quarter(mask):
        return lax.dynamic_slice_in_dim(part, jnp.bitwise_xor(place, mask) * rows, rows, 0)

    received = [swap(quarter(mask), 2 * mask) for mask in (1, 2, 3)]
    total = quarter(0) + received[0] + received[1] + received[2]
    for bit in range(3, bits):
        total = total + swap(total, 1 << bit)
    gathered = jnp.stack([total] + [swap(total, 2 * mask) for mask in (1, 2, 3)], axis=0)
    part = jnp.concatenate(
        [
            lax.dynamic_index_in_dim(gathered, jnp.bitwise_xor(place, at), 0, keepdims=False)
            for at in range(4)
        ],
        axis=0,
    )
    other = swap(part, 1)
    return jnp.concatenate([jnp.where(odd, other, part), jnp.where(odd, part, other)], axis=0)


def first_lanes(values, width):
    lane = lax.broadcasted_iota(jnp.int32, values.shape, 1)
    return jnp.where(lane < width, values, 0.0)


def product(left, right, across):
    dims = (((1,), (1 if across else 0,)), ((), ()))

    def one(a, b):
        return lax.dot_general(a, b, dims, preferred_element_type=jnp.float32)

    return one(left[0], right[0]) + (one(left[0], right[1]) + one(left[1], right[0]))


def core_kernel(
    packed_ref,
    core_ref,
    modes_hbm,
    snaps_hbm,
    new_hbm,
    core_out,
    captured_ref,
    energy_ref,
    norms_ref,
    inner_ref,
    snaps_ref,
    kept_ref,
    rows_ref,
    new_ref,
    in_sems,
    out_sems,
):
    loads = [pltpu.make_async_copy(modes_hbm, rows_ref.at[pl.ds(0, modes_hbm.shape[0])], in_sems.at[0])]
    for batch in range(snaps_hbm.shape[0]):
        at = modes_hbm.shape[0] + batch * snaps_hbm.shape[1]
        loads.append(
            pltpu.make_async_copy(
                snaps_hbm.at[batch], rows_ref.at[pl.ds(at, snaps_hbm.shape[1])], in_sems.at[1 + batch]
            )
        )
    for load in loads:
        load.start()
    rank = core_ref.shape[0]
    batches = captured_ref.shape[0]
    width = snaps_ref.shape[0] // batches
    probes = captured_ref.shape[1] - batches * width
    half = rank // 2
    norms_ref[:half, :half] = packed_ref[:half, :]
    norms_ref[half:, :half] = packed_ref[half:rank, :]
    norms_ref[:half, half:] = packed_ref[half:rank, :].T
    norms_ref[half:, half:] = packed_ref[rank:rank + half, :]
    at = rank + half
    for target_ref in (inner_ref, snaps_ref):
        count = target_ref.shape[0]
        for batch in range(batches):
            tile = slice(batch * LANES, (batch + 1) * LANES)
            if batch + 1 < batches:
                target_ref[:, tile] = packed_ref[at:at + count, :]
                at += count
            else:
                target_ref[:, tile] = unfold(packed_ref[at:at + count // 2, :])
                at += count // 2
    energy_ref[...] = nt(core_ref[...], core_ref[...])
    lane = lax.broadcasted_iota(jnp.int32, kept_ref.shape, 1)
    row = lax.broadcasted_iota(jnp.int32, kept_ref.shape, 0)
    kept_ref[...] = jnp.where(lane == row, 1.0, 0.0)
    spare = jnp.zeros((LANES - width, LANES), jnp.float32)

    def absorb(batch, carry):
        tile = pl.ds(pl.multiple_of(batch * LANES, LANES), LANES)
        own_rows = pl.ds(pl.multiple_of(batch * width, GROUP), width)
        own = jnp.concatenate([first_lanes(snaps_ref[own_rows, tile], width), spare], axis=0)
        projected = first_lanes(inner_ref[:, tile], width)
        projected_s = split(projected)
        norms = split(norms_ref[...])
        crossed = tn(projected, projected)
        residual = own - crossed - crossed + tn(projected, product(norms, projected_s, False))
        residual_s = split(residual)
        top = energy_ref[...] + product(projected_s, projected_s, True)
        top_s = split(top)
        coupling_s = split(product(projected_s, residual_s, False))
        gram = product(top_s, top_s, True) + product(coupling_s, projected_s, True)
        inverse = split(inverse_factor(gram))
        first_rows = split(product(inverse, top_s, False))
        first_low = split(product(inverse, projected_s, False))
        turned_rows = product(first_rows, top_s, False) + product(first_low, coupling_s, True)
        turned_low = product(first_rows, projected_s, False) + product(first_low, residual_s, False)
        gram = nt(turned_rows, turned_rows) + nt(nn(turned_low, residual), turned_low)
        inverse = inverse_factor(gram)
        rows = nn(inverse, turned_rows)
        low = nn(inverse, turned_low)
        rows_s = split(rows)
        low_s = split(low)
        low_residual = product(low_s, residual_s, False)
        applied_rows = product(rows_s, top_s, False) + product(low_s, coupling_s, True)
        applied_low = product(rows_s, projected_s, False) + low_residual
        energy_ref[...] = product(split(applied_rows), rows_s, True) + product(
            split(applied_low), split(low_residual), True
        )
        old = split(rows - product(low_s, projected_s, True))
        with_window = jnp.concatenate(
            [snaps_ref[own_rows, :], jnp.zeros((LANES - width, snaps_ref.shape[1]), jnp.float32)], axis=0
        )
        inner_ref[...] = product(old, split(inner_ref[...]), False) + product(low_s, split(with_window), False)
        across = product(old, norms, False) + product(low_s, projected_s, True)
        norms_ref[...] = product(split(across), old, True) + product(
            split(first_lanes(inner_ref[:, tile], width)), low_s, True
        )
        kept_ref[...] = product(old, split(kept_ref[...]), False)
        kept_ref[:, pl.ds(pl.multiple_of(rank + batch * LANES, LANES), LANES)] = low
        for number in range(batches):
            tile = inner_ref[:, number * LANES:(number + 1) * LANES]
            turned = jnp.concatenate([tile[at:at + LANES, :].T for at in range(0, rank, LANES)], axis=1)
            captured_ref[batch, number * width:(number + 1) * width, :] = turned[:width, :]
            room = LANES - width
            taken = min(max(probes - number * room, 0), room)
            if taken:
                at = batches * width + number * room
                captured_ref[batch, at:at + taken, :] = turned[width:width + taken, :]
        return carry

    lax.fori_loop(0, batches, absorb, 0)
    mix = jnp.concatenate(
        [kept_ref[:, :rank]]
        + [kept_ref[:, rank + b * LANES:rank + b * LANES + width] for b in range(batches)],
        axis=1,
    )
    mix_high, mix_low = split(mix)

    def one(left, right):
        return lax.dot_general(
            left, right, (((1,), (0,)), ((), ())), preferred_element_type=jnp.float32
        )

    for load in loads:
        load.wait()
    blocks = rank // PANEL
    columns = rows_ref.shape[1] // blocks
    piece = columns // (PANEL // GROUP)
    stores = []
    for number in range(blocks):
        start = number * PANEL
        end = start + PANEL
        steps = eliminate_panel(energy_ref[start:end, :], start, False)
        for part in range(PANEL // GROUP):
            at = number * columns + part * piece
            high, low = split(rows_ref[:, at:at + piece])
            new_ref[:, at:at + piece] = one(mix_high, high) + (one(mix_high, low) + one(mix_low, high))
            next(steps)
        block = pl.ds(number * columns, columns)
        stores.append(
            pltpu.make_async_copy(new_ref.at[:, block], new_hbm.at[:, block], out_sems.at[number])
        )
        stores[-1].start()
        panel = finish(steps)
        energy_ref[start:end, :] = panel
        if end < rank:
            energy_ref[end:, :] = energy_ref[end:, :] - stacked_square(panel, end)
    lane = lax.broadcasted_iota(jnp.int32, (rank, rank), 1)
    row = lax.broadcasted_iota(jnp.int32, (rank, rank), 0)
    core_out[...] = jnp.where(lane >= row, energy_ref[...], 0.0).T
    for store in stores:
        store.wait()


def updated(packed, core, modes, snaps, probes):
    rank, columns = modes.shape
    batches, width, _ = snaps.shape
    snap_count = batches * width
    tiles = batches * LANES
    whole = pl.BlockSpec(memory_space=pltpu.VMEM)
    apart = pl.BlockSpec(memory_space=pl.ANY)
    return pl.pallas_call(
        core_kernel,
        in_specs=[whole, whole, apart, apart],
        out_specs=[apart, whole, whole],
        out_shape=[
            jax.ShapeDtypeStruct((rank, columns), jnp.float32),
            jax.ShapeDtypeStruct((rank, rank), jnp.float32),
            jax.ShapeDtypeStruct((batches, snap_count + probes, rank), jnp.float32),
        ],
        scratch_shapes=[
            pltpu.VMEM((rank, rank), jnp.float32),
            pltpu.VMEM((rank, rank), jnp.float32),
            pltpu.VMEM((rank, tiles), jnp.float32),
            pltpu.VMEM((snap_count, tiles), jnp.float32),
            pltpu.VMEM((rank, rank + tiles), jnp.float32),
            pltpu.VMEM((rank + snap_count, columns), jnp.float32),
            pltpu.VMEM((rank, columns), jnp.float32),
            pltpu.SemaphoreType.DMA((1 + batches,)),
            pltpu.SemaphoreType.DMA((rank // PANEL,)),
        ],
        compiler_params=pltpu.CompilerParams(vmem_limit_bytes=52 << 20),
        name="core_updates",
    )(packed, core, modes, snaps)


def body(modes, snaps, probes, core, *, devices):
    rank, columns = modes.shape
    batches, width, _ = snaps.shape
    scale = 1.0 / (columns * devices)
    packed = sum_over_devices(local_grams(modes, snaps, probes, scale), devices)
    new_modes, new_core, captured = updated(packed, core, modes, snaps, probes.shape[0])
    return new_modes, new_core, jnp.swapaxes(captured, 1, 2)


def solution(mesh):
    devices = mesh.shape["space"] * mesh.shape["sub"]
    return jax.shard_map(
        functools.partial(body, devices=devices),
        mesh=mesh,
        in_specs=(P(None, AXES), P(None, None, AXES), P(None, AXES), P()),
        out_specs=(P(None, AXES), P(), P()),
        check_vma=False,
    )
```

```python
import functools

import jax
import jax.numpy as jnp
from jax import lax
from jax.experimental import pallas as pl
from jax.experimental.pallas import tpu as pltpu
from jax.sharding import PartitionSpec as P

TURNS = 2
AXES = ("space", "sub")
FULL = lax.Precision.HIGHEST
LANES = 128
GROUP = 8
PANEL = 32


def nn(left, right):
    return lax.dot_general(
        left, right, (((1,), (0,)), ((), ())), precision=FULL, preferred_element_type=jnp.float32
    )


def nt(left, right):
    return lax.dot_general(
        left, right, (((1,), (1,)), ((), ())), precision=FULL, preferred_element_type=jnp.float32
    )


def tn(left, right):
    return lax.dot_general(
        left, right, (((0,), (0,)), ((), ())), precision=FULL, preferred_element_type=jnp.float32
    )


def wide(column, order):
    return jnp.concatenate([column] * (order // LANES), axis=1)


def eliminate_panel(block, start, inverting):
    size, order = block.shape
    lane = lax.broadcasted_iota(jnp.int32, (GROUP, order), 1)
    row = lax.broadcasted_iota(jnp.int32, (GROUP, order), 0)
    row_one = lax.broadcasted_iota(jnp.int32, (GROUP, LANES), 0)
    groups = size // GROUP
    held = [block[g * GROUP:(g + 1) * GROUP, :] for g in range(groups)]
    panel = []

    def spread(first, g0):
        return [
            [
                jnp.broadcast_to(held[g][:, first + j:first + j + 1], (GROUP, LANES))
                for g in range(g0, groups)
            ]
            for j in range(GROUP)
        ]

    own = spread(start, 0)
    for g0 in range(groups):
        first = start + g0 * GROUP
        ahead = spread(first + GROUP, g0) if g0 + 1 < groups else []
        if inverting:
            inside = (lane >= first) & (lane < first + GROUP)
            held[g0] = jnp.where(inside, jnp.where(lane - first == row, 1.0, 0.0), held[g0])
            for g in range(g0 + 1, groups):
                held[g] = jnp.where(inside, 0.0, held[g])
        pivot_column = jnp.ones((GROUP, LANES), jnp.float32)
        factors = []
        for j in range(GROUP):
            pivot = jnp.broadcast_to(own[j][0][j:j + 1, :], (GROUP, LANES))
            inverse = pltpu.reciprocal(pivot, approx=True)
            pivot_column = jnp.where(row_one == j, pivot, pivot_column)
            factor = [column * inverse for column in own[j]]
            for column in own[j + 1:] + ahead:
                across = jnp.broadcast_to(column[0][j:j + 1, :], (GROUP, LANES))
                for t in range(groups - g0):
                    column[t] = column[t] - factor[t] * across
            factor[0] = jnp.where(row_one > j, factor[0], 0.0)
            factors.append(factor)
        for j in range(GROUP):
            pivot_row = jnp.broadcast_to(held[g0][j:j + 1, :], (GROUP, order))
            for t in range(groups - g0):
                held[g0 + t] = held[g0 + t] - wide(factors[j][t], order) * pivot_row
        panel.append(held[g0] * wide(lax.rsqrt(pivot_column), order))
        own = [column[1:] for column in ahead]
        yield
    if inverting:
        panel = [
            jnp.where((lane >= start + GROUP * (g + 1)) & (lane < start + size), 0.0, panel[g])
            for g in range(groups)
        ]
    return jnp.concatenate(panel, axis=0)


def finish(steps):
    while True:
        try:
            next(steps)
        except StopIteration as done:
            return done.value


def stacked_square(panel, begin):
    high = panel.astype(jnp.bfloat16)
    left = panel - high.astype(jnp.float32)
    mid = left.astype(jnp.bfloat16)
    low = (left - mid.astype(jnp.float32)).astype(jnp.bfloat16)
    first = jnp.concatenate([high, high, mid, mid, high, low], axis=0)
    second = jnp.concatenate([high, mid, high, mid, low, high], axis=0)
    return lax.dot_general(
        first[:, begin:], second, (((0,), (0,)), ((), ())), preferred_element_type=jnp.float32
    )


def inverse_factor(matrix):
    order = matrix.shape[0]
    finished = []
    for start in range(0, order, PANEL):
        end = start + PANEL
        panel = finish(eliminate_panel(matrix[:PANEL, :], start, True))
        finished.append(panel)
        if end < order:
            rest = matrix[PANEL:, :]
            rest_lane = lax.broadcasted_iota(jnp.int32, rest.shape, 1)
            rest = jnp.where((rest_lane >= start) & (rest_lane < end), 0.0, rest)
            matrix = rest - stacked_square(panel, end)
    lowered = jnp.concatenate(finished, axis=0)
    lane = lax.broadcasted_iota(jnp.int32, lowered.shape, 1)
    row = lax.broadcasted_iota(jnp.int32, lowered.shape, 0)
    return jnp.where(lane <= row, lowered, 0.0)


def split(values):
    high = values.astype(jnp.bfloat16)
    low = (values - high.astype(jnp.float32)).astype(jnp.bfloat16)
    return high, low


def nt_pass(left, right):
    return lax.dot_general(
        left, right, (((1,), (1,)), ((), ())), preferred_element_type=jnp.float32
    )


def packed_rows(rank, snap_count, batches):
    own = 3 * (rank // 2)
    rows = own + (rank + snap_count) * (batches - 1) + (rank + snap_count) // 2
    return -(-rows // (8 * GROUP)) * (8 * GROUP)


def fold(block):
    half = block.shape[0] // 2
    return jnp.concatenate([block[:half, :LANES // 2], block[half:, :LANES // 2]], axis=1)


def unfold(block):
    zeros = jnp.zeros((block.shape[0], LANES // 2), jnp.float32)
    return jnp.concatenate(
        [
            jnp.concatenate([block[:, :LANES // 2], zeros], axis=1),
            jnp.concatenate([block[:, LANES // 2:], zeros], axis=1),
        ],
        axis=0,
    )


def gram_kernel(
    scale, modes_ref, snaps_ref, probes_ref, packed_ref, norms_out, cross_out, past_snaps, past_probes, own_out, own_cross, others_out
):
    step = pl.program_id(0)
    sums = (norms_out, cross_out, past_snaps, past_probes, own_out, own_cross, others_out)

    @pl.when(step == 0)
    def _():
        for ref in sums:
            ref[...] = jnp.zeros_like(ref)

    rank, columns = modes_ref.shape
    count, width, _ = snaps_ref.shape
    snap_count = count * width
    probe_count = probes_ref.shape[0]
    high, low = split(modes_ref[...])
    snap_high, snap_low = split(snaps_ref[...].reshape(snap_count, columns))
    probe_high, probe_low = split(probes_ref[...])
    norms_out[...] += nt_pass(high, high)
    cross_out[...] += nt_pass(low, high)
    past_snaps[...] += nt_pass(snap_high, high) + (nt_pass(snap_low, high) + nt_pass(snap_high, low))
    past_probes[...] += nt_pass(probe_high, high) + (nt_pass(probe_low, high) + nt_pass(probe_high, low))
    own_out[...] += nt_pass(snap_high, snap_high)
    own_cross[...] += nt_pass(snap_low, snap_high)
    others_out[...] += nt_pass(probe_high, snap_high) + (
        nt_pass(probe_low, snap_high) + nt_pass(probe_high, snap_low)
    )

    @pl.when(step == pl.num_programs(0) - 1)
    def _():
        half = rank // 2
        spare = LANES - width
        cross = cross_out[...]
        norms = norms_out[...] + (cross + cross.T)
        blocks = [norms[:half, :half], norms[half:, :half], norms[half:, half:]]
        for batch in range(count):
            tile = [past_snaps[batch * width:(batch + 1) * width, :]]
            taken = min(max(probe_count - batch * spare, 0), spare)
            if taken:
                tile.append(past_probes[batch * spare:batch * spare + taken, :])
            if taken < spare:
                tile.append(jnp.zeros((spare - taken, rank), jnp.float32))
            tile = jnp.concatenate(tile, axis=0)
            block = jnp.concatenate([tile[:, :half].T, tile[:, half:].T], axis=0)
            blocks.append(block if batch + 1 < count else fold(block))
        cross = jnp.concatenate(
            [own_cross[...], jnp.zeros((snap_count, rank - snap_count), jnp.float32)], axis=1
        )
        cross = jnp.concatenate([cross, jnp.zeros((rank - snap_count, rank), jnp.float32)], axis=0)
        others = jnp.concatenate(
            [others_out[...], jnp.zeros((probe_count, rank - snap_count), jnp.float32)], axis=1
        )
        others = jnp.concatenate([others[:, :half].T, others[:, half:].T], axis=0)[:snap_count, :]
        own = own_out[...] + (own_cross[...] + cross.T[:snap_count, :snap_count])
        for batch in range(count):
            tile = [own[:, batch * width:(batch + 1) * width]]
            taken = min(max(probe_count - batch * spare, 0), spare)
            if taken:
                tile.append(others[:, batch * spare:batch * spare + taken])
            if taken < spare:
                tile.append(jnp.zeros((snap_count, spare - taken), jnp.float32))
            block = jnp.concatenate(tile, axis=1)
            blocks.append(block if batch + 1 < count else fold(block))
        at = 0
        for block in blocks:
            packed_ref[at:at + block.shape[0], :] = block * scale
            at += block.shape[0]
        if at < packed_ref.shape[0]:
            packed_ref[at:, :] = jnp.zeros((packed_ref.shape[0] - at, LANES), jnp.float32)


def local_grams(modes, snaps, probes, scale):
    rank, columns = modes.shape
    count, width, _ = snaps.shape
    probe_count = probes.shape[0]
    tile = 1024
    rows = packed_rows(rank, count * width, count)
    return pl.pallas_call(
        functools.partial(gram_kernel, scale),
        grid=(columns // tile,),
        in_specs=[
            pl.BlockSpec((rank, tile), lambda i: (0, i)),
            pl.BlockSpec((count, width, tile), lambda i: (0, 0, i)),
            pl.BlockSpec((probe_count, tile), lambda i: (0, i)),
        ],
        out_specs=pl.BlockSpec((rows, LANES), lambda i: (0, 0)),
        out_shape=jax.ShapeDtypeStruct((rows, LANES), jnp.float32),
        scratch_shapes=[
            pltpu.VMEM(shape, jnp.float32)
            for shape in (
                (rank, rank), (rank, rank), (count * width, rank), (probe_count, rank),
                (count * width, count * width), (count * width, count * width), (probe_count, count * width),
            )
        ],
        compiler_params=pltpu.CompilerParams(vmem_limit_bytes=60 << 20),
        name="grams",
    )(modes, snaps, probes)


def sum_over_devices(part, size):
    def swap(value, mask):
        return lax.ppermute(value, AXES, [(i, i ^ mask) for i in range(size)])

    bits = size.bit_length() - 1
    if size != 1 << bits or bits < 3 or part.shape[0] % (8 * GROUP):
        return lax.psum(part, AXES)
    index = lax.axis_index(AXES)
    core = lax.rem(index, 2)
    odd = core == 1
    half = part.shape[0] // 2
    away = swap(lax.dynamic_slice_in_dim(part, (1 - core) * half, half, 0), 1)
    part = lax.dynamic_slice_in_dim(part, core * half, half, 0) + away
    place = lax.rem(lax.div(index, 2), 4)
    rows = half // 4

    def quarter(mask):
        return lax.dynamic_slice_in_dim(part, jnp.bitwise_xor(place, mask) * rows, rows, 0)

    received = [swap(quarter(mask), 2 * mask) for mask in (1, 2, 3)]
    total = quarter(0) + received[0] + received[1] + received[2]
    for bit in range(3, bits):
        total = total + swap(total, 1 << bit)
    gathered = jnp.stack([total] + [swap(total, 2 * mask) for mask in (1, 2, 3)], axis=0)
    part = jnp.concatenate(
        [
            lax.dynamic_index_in_dim(gathered, jnp.bitwise_xor(place, at), 0, keepdims=False)
            for at in range(4)
        ],
        axis=0,
    )
    other = swap(part, 1)
    return jnp.concatenate([jnp.where(odd, other, part), jnp.where(odd, part, other)], axis=0)


def first_lanes(values, width):
    lane = lax.broadcasted_iota(jnp.int32, values.shape, 1)
    return jnp.where(lane < width, values, 0.0)


def product(left, right, across):
    dims = (((1,), (1 if across else 0,)), ((), ()))

    def one(a, b):
        return lax.dot_general(a, b, dims, preferred_element_type=jnp.float32)

    return one(left[0], right[0]) + (one(left[0], right[1]) + one(left[1], right[0]))


def core_kernel(
    packed_ref,
    core_ref,
    modes_hbm,
    snaps_hbm,
    new_hbm,
    core_out,
    captured_ref,
    energy_ref,
    norms_ref,
    inner_ref,
    snaps_ref,
    kept_ref,
    rows_ref,
    new_ref,
    in_sems,
    out_sems,
):
    loads = [pltpu.make_async_copy(modes_hbm, rows_ref.at[pl.ds(0, modes_hbm.shape[0])], in_sems.at[0])]
    for batch in range(snaps_hbm.shape[0]):
        at = modes_hbm.shape[0] + batch * snaps_hbm.shape[1]
        loads.append(
            pltpu.make_async_copy(
                snaps_hbm.at[batch], rows_ref.at[pl.ds(at, snaps_hbm.shape[1])], in_sems.at[1 + batch]
            )
        )
    for load in loads:
        load.start()
    rank = core_ref.shape[0]
    batches = captured_ref.shape[0]
    width = snaps_ref.shape[0] // batches
    probes = captured_ref.shape[1] - batches * width
    half = rank // 2
    norms_ref[:half, :half] = packed_ref[:half, :]
    norms_ref[half:, :half] = packed_ref[half:rank, :]
    norms_ref[:half, half:] = packed_ref[half:rank, :].T
    norms_ref[half:, half:] = packed_ref[rank:rank + half, :]
    at = rank + half
    for target_ref in (inner_ref, snaps_ref):
        count = target_ref.shape[0]
        for batch in range(batches):
            tile = slice(batch * LANES, (batch + 1) * LANES)
            if batch + 1 < batches:
                target_ref[:, tile] = packed_ref[at:at + count, :]
                at += count
            else:
                target_ref[:, tile] = unfold(packed_ref[at:at + count // 2, :])
                at += count // 2
    energy_ref[...] = nt(core_ref[...], core_ref[...])
    lane = lax.broadcasted_iota(jnp.int32, kept_ref.shape, 1)
    row = lax.broadcasted_iota(jnp.int32, kept_ref.shape, 0)
    kept_ref[...] = jnp.where(lane == row, 1.0, 0.0)
    spare = jnp.zeros((LANES - width, LANES), jnp.float32)

    def absorb(batch, carry):
        tile = pl.ds(pl.multiple_of(batch * LANES, LANES), LANES)
        own_rows = pl.ds(pl.multiple_of(batch * width, GROUP), width)
        own = jnp.concatenate([first_lanes(snaps_ref[own_rows, tile], width), spare], axis=0)
        projected = first_lanes(inner_ref[:, tile], width)
        projected_s = split(projected)
        norms = split(norms_ref[...])
        crossed = tn(projected, projected)
        residual = own - crossed - crossed + tn(projected, product(norms, projected_s, False))
        residual_s = split(residual)
        top = energy_ref[...] + product(projected_s, projected_s, True)
        top_s = split(top)
        coupling_s = split(product(projected_s, residual_s, False))
        gram = product(top_s, top_s, True) + product(coupling_s, projected_s, True)
        inverse = split(inverse_factor(gram))
        first_rows = split(product(inverse, top_s, False))
        first_low = split(product(inverse, projected_s, False))
        turned_rows = product(first_rows, top_s, False) + product(first_low, coupling_s, True)
        turned_low = product(first_rows, projected_s, False) + product(first_low, residual_s, False)
        gram = nt(turned_rows, turned_rows) + nt(nn(turned_low, residual), turned_low)
        inverse = inverse_factor(gram)
        rows = nn(inverse, turned_rows)
        low = nn(inverse, turned_low)
        rows_s = split(rows)
        low_s = split(low)
        low_residual = product(low_s, residual_s, False)
        applied_rows = product(rows_s, top_s, False) + product(low_s, coupling_s, True)
        applied_low = product(rows_s, projected_s, False) + low_residual
        energy_ref[...] = product(split(applied_rows), rows_s, True) + product(
            split(applied_low), split(low_residual), True
        )
        old = split(rows - product(low_s, projected_s, True))
        with_window = jnp.concatenate(
            [snaps_ref[own_rows, :], jnp.zeros((LANES - width, snaps_ref.shape[1]), jnp.float32)], axis=0
        )
        inner_ref[...] = product(old, split(inner_ref[...]), False) + product(low_s, split(with_window), False)
        across = product(old, norms, False) + product(low_s, projected_s, True)
        norms_ref[...] = product(split(across), old, True) + product(
            split(first_lanes(inner_ref[:, tile], width)), low_s, True
        )
        kept_ref[...] = product(old, split(kept_ref[...]), False)
        kept_ref[:, pl.ds(pl.multiple_of(rank + batch * LANES, LANES), LANES)] = low
        for number in range(batches):
            tile = inner_ref[:, number * LANES:(number + 1) * LANES]
            turned = jnp.concatenate([tile[at:at + LANES, :].T for at in range(0, rank, LANES)], axis=1)
            captured_ref[batch, number * width:(number + 1) * width, :] = turned[:width, :]
            room = LANES - width
            taken = min(max(probes - number * room, 0), room)
            if taken:
                at = batches * width + number * room
                captured_ref[batch, at:at + taken, :] = turned[width:width + taken, :]
        return carry

    lax.fori_loop(0, batches, absorb, 0)
    mix = jnp.concatenate(
        [kept_ref[:, :rank]]
        + [kept_ref[:, rank + b * LANES:rank + b * LANES + width] for b in range(batches)],
        axis=1,
    )
    mix_high, mix_low = split(mix)

    def one(left, right):
        return lax.dot_general(
            left, right, (((1,), (0,)), ((), ())), preferred_element_type=jnp.float32
        )

    for load in loads:
        load.wait()
    blocks = rank // PANEL
    columns = rows_ref.shape[1] // blocks
    piece = columns // (PANEL // GROUP)
    stores = []
    for number in range(blocks):
        start = number * PANEL
        end = start + PANEL
        steps = eliminate_panel(energy_ref[start:end, :], start, False)
        for part in range(PANEL // GROUP):
            at = number * columns + part * piece
            high, low = split(rows_ref[:, at:at + piece])
            new_ref[:, at:at + piece] = one(mix_high, high) + (one(mix_high, low) + one(mix_low, high))
            next(steps)
        block = pl.ds(number * columns, columns)
        stores.append(
            pltpu.make_async_copy(new_ref.at[:, block], new_hbm.at[:, block], out_sems.at[number])
        )
        stores[-1].start()
        panel = finish(steps)
        energy_ref[start:end, :] = panel
        if end < rank:
            energy_ref[end:, :] = energy_ref[end:, :] - stacked_square(panel, end)
    lane = lax.broadcasted_iota(jnp.int32, (rank, rank), 1)
    row = lax.broadcasted_iota(jnp.int32, (rank, rank), 0)
    core_out[...] = jnp.where(lane >= row, energy_ref[...], 0.0).T
    for store in stores:
        store.wait()


def updated(packed, core, modes, snaps, probes):
    rank, columns = modes.shape
    batches, width, _ = snaps.shape
    snap_count = batches * width
    tiles = batches * LANES
    whole = pl.BlockSpec(memory_space=pltpu.VMEM)
    apart = pl.BlockSpec(memory_space=pl.ANY)
    return pl.pallas_call(
        core_kernel,
        in_specs=[whole, whole, apart, apart],
        out_specs=[apart, whole, whole],
        out_shape=[
            jax.ShapeDtypeStruct((rank, columns), jnp.float32),
            jax.ShapeDtypeStruct((rank, rank), jnp.float32),
            jax.ShapeDtypeStruct((batches, snap_count + probes, rank), jnp.float32),
        ],
        scratch_shapes=[
            pltpu.VMEM((rank, rank), jnp.float32),
            pltpu.VMEM((rank, rank), jnp.float32),
            pltpu.VMEM((rank, tiles), jnp.float32),
            pltpu.VMEM((snap_count, tiles), jnp.float32),
            pltpu.VMEM((rank, rank + tiles), jnp.float32),
            pltpu.VMEM((rank + snap_count, columns), jnp.float32),
            pltpu.VMEM((rank, columns), jnp.float32),
            pltpu.SemaphoreType.DMA((1 + batches,)),
            pltpu.SemaphoreType.DMA((rank // PANEL,)),
        ],
        compiler_params=pltpu.CompilerParams(vmem_limit_bytes=52 << 20),
        name="core_updates",
    )(packed, core, modes, snaps)


def body(modes, snaps, probes, core, *, devices):
    rank, columns = modes.shape
    batches, width, _ = snaps.shape
    scale = 1.0 / (columns * devices)
    packed = sum_over_devices(local_grams(modes, snaps, probes, scale), devices)
    new_modes, new_core, captured = updated(packed, core, modes, snaps, probes.shape[0])
    return new_modes, new_core, jnp.swapaxes(captured, 1, 2)


def solution(mesh):
    devices = mesh.shape["space"] * mesh.shape["sub"]
    return jax.shard_map(
        functools.partial(body, devices=devices),
        mesh=mesh,
        in_specs=(P(None, AXES), P(None, None, AXES), P(None, AXES), P()),
        out_specs=(P(None, AXES), P(), P()),
        check_vma=False,
    )
```
